32 devices in a mesh: groups: 2 (over y), seq: 16 (over z, x, core).
Axes of the slice: x: 2, y: 2, z: 4, core: 2. Of those that a mesh axis runs over, the one named last changes fastest.
Arguments:
- queries: bfloat16 [4096, 2048], P(('groups', 'seq')), parts along dimension 0, may hold values from -240 to 240, as said below
- encodings: bfloat16 [64, 128, 1024], P('groups', 'seq'), parts along dimension 0, may hold values from -6 to 6
- neighbour_ids: int32 [64, 2], P(('groups', 'seq')), parts along dimension 0, may hold values from 0 to 31
- lengths: int32 [4], P('groups'), parts along dimension 0, may hold values from 64 to 1024, as said below
- w_key: bfloat16 [1024, 2048], replicated, may hold values from -0.1875 to 0.1875
- w_value: bfloat16 [1024, 2048], replicated, may hold values from -0.1875 to 0.1875
Outputs:
- attended: bfloat16 [4096, 2048], P(('groups', 'seq')), parts along dimension 0
The draws below stay inside these ranges and needn't reach their ends.
There are 2 independent parts, one for each index of `groups`. The reference program is written for one: setup_inputs(seed, part) draws one part's arguments, and reference() takes and returns one part's arrays. A program takes and returns all parts, laid end to end along the dimension named above; an argument that names none is the same for every part. Nothing has to cross between parts.
Inputs may be any that keep to these rules, and one draw needn't show every extreme that they name: `queries`: queries are of order one in the shown draw; rows may have unlike scales. `lengths`: each length is a multiple of nothing in particular; some prompt fills its room of 1024 tokens.
All inputs are finite; a program needn't handle non-finite values.
Results may differ from the reference program's by a relative error of at most 0.012.
The reference program's roundings to bfloat16 on the way (of `keys`, `values` and `weights`) count: a program that leaves them out, or rounds other values in their place, can miss the bound.
Values may be sent and summed in bfloat16 or wider, within the bound.
A program may use at most 64 MiB of HBM per device.

```python
import math
import jax
import jax.numpy as jnp
import numpy as np
from jax import lax

HEADS = 16
DH = 128
HD = 2048
ENC = 1024
NTOK = 128
PROMPTS = 2
TOKENS = 2048
SLOT = 1024
SPANS = 32
NEIGH = 32


def draw_queries(key, part):
    key = jax.random.fold_in(key, 11)
    first = jax.random.fold_in(key, 0)
    values = jnp.clip(jax.random.normal(first, (TOKENS, HD), jnp.float32), -6.0, 6.0)
    return values.astype(jnp.bfloat16)


def draw_lengths(key, part):
    key = jax.random.fold_in(key, 23)
    first, second = jax.random.split(key)
    drawn = jax.random.randint(first, (PROMPTS,), 64, SLOT + 1, jnp.int32)
    chosen = jax.random.randint(second, (), 0, PROMPTS, jnp.int32)
    return jnp.where(jnp.arange(PROMPTS, dtype=jnp.int32) == chosen, SLOT, drawn).astype(jnp.int32)


def set_ends(array, stream_key, low, top_value):
    longest = array.shape.index(max(array.shape))
    spots = []
    for shift in (0, 1):
        where = [jax.random.randint(jax.random.fold_in(stream_key, axis), (), 0, length) for axis, length in enumerate(array.shape)]
        where[longest] = (where[longest] + shift) % array.shape[longest]
        spots.append(tuple(where))
    return array.at[spots[0]].set(low).at[spots[1]].set(top_value)


def block_scale(rng, shape, shards, smallest, largest):
    gain = 1.0
    for dim, shards_of in shards:
        draws = jax.random.uniform(jax.random.fold_in(jax.random.fold_in(rng, 6), dim), (shards_of,), jnp.float32, smallest / len(shards), largest / len(shards))
        gain = gain * jnp.repeat(jnp.exp(draws), shape[dim] // shards_of).reshape((-1,) + (1,) * (len(shape) - 1 - dim))
    return gain


def rank_bounds(count, skew):
    portions = [(1 << 20) // math.isqrt(standing ** skew) + 1 for standing in range(1, count + 1)]
    scale = 1 + sum(portions) // (1 << 30)
    return np.cumsum(np.array([max(1, weight // scale) for weight in portions]))


def ranked_ids(key, extent, number_of, slope):
    table = rank_bounds(number_of, slope)
    lot = jax.random.randint(jax.random.fold_in(key, 1), extent, 0, int(table[number_of - 1]))
    grade = jnp.searchsorted(jnp.asarray(table, jnp.int32), lot, side="right")
    return jax.random.permutation(jax.random.fold_in(key, 2), number_of)[grade].astype(jnp.int32)


def bell_draw(rng, extent, width, most, shards=(), kind=jnp.bfloat16):
    entries = width * jax.random.normal(rng, extent, jnp.float32)
    if shards:
        entries = entries * block_scale(rng, extent, shards, -0.22, 0.18)
    return jnp.clip(entries, -most, most).astype(kind)


def setup_inputs(seed: int = 0, part: int = 0) -> dict:
    arg_keys = jax.random.split(jax.random.key(seed), 7)
    own_keys = jax.random.split(jax.random.fold_in(arg_keys[6], part), 7)
    queries = draw_queries(jax.random.fold_in(jax.random.fold_in(arg_keys[6], part), 71), part)
    encodings = bell_draw(own_keys[1], (NEIGH, NTOK, ENC), 1.0, 6.0, ((1, 16),))
    neighbour_ids = set_ends(ranked_ids(own_keys[2], (SPANS, 2), NEIGH, 2), jax.random.fold_in(own_keys[2], 3), 0, NEIGH - 1).astype(jnp.int32)
    lengths = draw_lengths(jax.random.fold_in(jax.random.fold_in(arg_keys[6], part), 71), part)
    w_key = bell_draw(arg_keys[4], (ENC, HD), ENC ** -0.5, 0.1875)
    w_value = bell_draw(arg_keys[5], (ENC, HD), ENC ** -0.5, 0.1875)
    return dict(queries=queries, encodings=encodings, neighbour_ids=neighbour_ids, lengths=lengths, w_key=w_key, w_value=w_value)


def reference(queries, encodings, neighbour_ids, lengths, w_key, w_value):
    def project(block):
        key_rows = jnp.dot(block, w_key, preferred_element_type=jnp.float32).astype(jnp.bfloat16)
        value_rows = jnp.dot(block, w_value, preferred_element_type=jnp.float32).astype(jnp.bfloat16)
        return key_rows, value_rows

    keys, values = lax.map(project, encodings)
    padded = jnp.concatenate([queries, jnp.zeros((64, HD), queries.dtype)], 0)
    scale = 1.0 / (DH ** 0.5)

    def attend_span(span):
        start = (span * 64 + 63).astype(jnp.int32)
        rows = lax.dynamic_slice_in_dim(padded, start, 64, 0)
        picked = neighbour_ids[span]
        key_set = keys[picked].reshape(2 * NTOK, HEADS, DH).astype(jnp.float32)
        value_set = values[picked].reshape(2 * NTOK, HEADS, DH).astype(jnp.float32)
        query_set = rows.reshape(64, HEADS, DH).astype(jnp.float32)
        scores = jnp.einsum("thd,khd->htk", query_set, key_set) * scale
        top = jnp.max(scores, axis=2, keepdims=True)
        expo = jnp.exp(scores - top)
        weights = (expo / jnp.sum(expo, axis=2, keepdims=True)).astype(jnp.bfloat16)
        result = jnp.einsum("htk,khd->thd", weights.astype(jnp.float32), value_set)
        return result.reshape(64, HD)

    blocks = lax.map(attend_span, jnp.arange(SPANS, dtype=jnp.int32))
    flat = blocks.reshape(SPANS * 64, HD)
    full = jnp.concatenate([jnp.zeros((63, HD), jnp.float32), flat[:TOKENS - 63]], 0)
    positions = jnp.arange(TOKENS, dtype=jnp.int32)
    within = positions % SLOT
    prompt = positions // SLOT
    limit = lengths[prompt]
    live = (within >= 63) & (within < limit)
    return jnp.where(live[:, None], full, 0.0).astype(jnp.bfloat16)
```

```python
import functools
import jax
import jax.numpy as jnp
from jax import lax
from jax.experimental import pallas as pl
from jax.experimental.pallas import tpu as pltpu
from jax.sharding import PartitionSpec as P

HEADS = 16
DH = 128
SPAN = 64


def general_body(queries, encodings, neighbour_ids, lengths, w_key, w_value):
    seq_count = lax.axis_size("seq")
    position = lax.axis_index("seq")
    tok_rows, width = queries.shape
    blocks = tok_rows // 64
    slots = blocks + 1
    enc_width = encodings.shape[2]
    id_all = lax.all_gather(neighbour_ids, "seq", axis=0, tiled=True)
    total_spans = id_all.shape[0]
    wanted_span = (
        jnp.arange(seq_count, dtype=jnp.int32)[:, None] * blocks
        - 1
        + jnp.arange(slots, dtype=jnp.int32)[None, :]
    )
    wanted_span = jnp.clip(wanted_span, 0, total_spans - 1)
    wanted = id_all[wanted_span].reshape(seq_count, 2 * slots)
    outgoing = encodings[wanted]
    block = lax.all_to_all(outgoing, "seq", split_axis=0, concat_axis=2, tiled=True)
    flat = block.reshape(-1, enc_width)
    shape = block.shape[:3] + (width,)
    key_rows = (
        jnp.dot(flat, w_key, preferred_element_type=jnp.float32).astype(jnp.bfloat16).reshape(shape)
    )
    value_rows = (
        jnp.dot(flat, w_value, preferred_element_type=jnp.float32)
        .astype(jnp.bfloat16)
        .reshape(shape)
    )
    ntok = key_rows.shape[2]
    key_total = key_rows.shape[1] * ntok
    key_set = key_rows.reshape(key_total, HEADS, DH)
    value_set = value_rows.reshape(key_total, HEADS, DH)
    key_slot = jnp.arange(key_total, dtype=jnp.int32) // (2 * ntok)
    local_rows = jnp.arange(tok_rows, dtype=jnp.int32)
    token_slot = (local_rows + 1) // 64
    allowed = token_slot[:, None] == key_slot[None, :]
    query_set = queries.reshape(tok_rows, HEADS, DH)
    scale = 1.0 / DH**0.5
    scores = (
        jnp.einsum("thd,khd->htk", query_set, key_set, preferred_element_type=jnp.float32) * scale
    )
    scores = jnp.where(allowed[None, :, :], scores, -1e30)
    top = jnp.max(scores, axis=2, keepdims=True)
    expo = jnp.where(allowed[None, :, :], jnp.exp(scores - top), 0.0)
    weights = (expo / jnp.sum(expo, axis=2, keepdims=True)).astype(jnp.bfloat16)
    result = jnp.einsum(
        "htk,khd->thd", weights, value_set, preferred_element_type=jnp.float32
    ).reshape(tok_rows, width)
    slot_room = tok_rows * seq_count // lengths.shape[0]
    global_rows = position * tok_rows + local_rows
    within = global_rows % slot_room
    prompt = global_rows // slot_room
    limit = jnp.sum(
        jnp.where(
            prompt[:, None] == jnp.arange(lengths.shape[0], dtype=jnp.int32)[None, :],
            lengths[None, :],
            0,
        ),
        axis=1,
    )
    live = (within >= 63) & (within < limit)
    return jnp.where(live[:, None], result, 0.0).astype(jnp.bfloat16)


def flipped(index, offset):
    bit = 1
    while bit <= offset:
        if offset & bit:
            index = index + bit - 2 * bit * ((index // bit) % 2)
        bit *= 2
    return index


def kernel(
    count,
    toks,
    ids_ref,
    q_ref,
    enc_hbm,
    wk_hbm,
    wv_hbm,
    out_ref,
    enc_ref,
    wk_ref,
    wv_ref,
    id_send,
    id_recv,
    send_buf,
    recv_buf,
    q_send,
    q_recv,
    q_shift,
    k_buf,
    v_buf,
    result,
    row_send,
    row_recv,
    local_sem,
    id_ssem,
    id_rsem,
    x_ssem,
    x_rsem,
    row_ssem,
    row_rsem,
):
    me = lax.axis_index("seq")
    following = lax.rem(me + 1, count)
    previous = lax.rem(me + count - 1, count)
    rows = 2 * toks
    total = count * rows
    enc_width = enc_ref.shape[1]
    width = q_ref.shape[1]
    offsets = sorted(range(1, count), reverse=True)

    def local(source, target, index):
        copy = pltpu.make_async_copy(source, target, local_sem.at[index])
        copy.start()
        return copy

    def remote(source, target, send_sem, recv_sem, device):
        return pltpu.make_async_remote_copy(
            src_ref=source,
            dst_ref=target,
            send_sem=send_sem,
            recv_sem=recv_sem,
            device_id={"seq": device},
            device_id_type=pl.DeviceIdType.MESH,
        )

    barrier = pltpu.get_barrier_semaphore()
    for offset in offsets:
        pl.semaphore_signal(
            barrier,
            inc=1,
            device_id={"seq": flipped(me, offset)},
            device_id_type=pl.DeviceIdType.MESH,
        )
    enc_copy = local(enc_hbm, enc_ref, 0)
    wk_copy = local(wk_hbm, wk_ref, 1)
    wv_copy = local(wv_hbm, wv_ref, 2)

    lane = lax.broadcasted_iota(jnp.int32, (1, 128), 1)
    mine = jnp.zeros((1, 128), jnp.float32)
    for span in range(2):
        for which in range(2):
            value = ids_ref[span, which].astype(jnp.float32)
            mine = jnp.where(lane == me * 4 + span * 2 + which, value, mine)
    id_send[...] = mine
    id_recv[me] = mine
    last = q_ref.shape[0] - 1
    q_send[...] = q_ref[last - 15 :, :].astype(jnp.float32)[15:, :]

    pl.semaphore_wait(barrier, count - 1)

    id_copies = {}
    for offset in offsets:
        id_copies[offset] = remote(
            id_send, id_recv.at[me], id_ssem.at[offset], id_rsem.at[offset], flipped(me, offset)
        )
        id_copies[offset].start()
    q_copy = remote(q_send, q_recv, row_ssem.at[0], row_rsem.at[0], following)
    q_copy.start()
    enc_copy.wait()
    for offset in offsets:
        id_copies[offset].wait_recv()
    ids = jnp.sum(id_recv[...], axis=0)

    x_copies = {}
    for slot in range(2):
        row = lax.broadcasted_iota(jnp.int32, (total, 128), 0)
        lanes = lax.broadcasted_iota(jnp.int32, (total, 128), 1)
        peer = row // rows
        which = (row % rows) // toks
        if slot == 0:
            origin = lax.rem(peer + count - 1, count) * 4 + 2 + which
        else:
            origin = peer * 4 + which
        chosen = jnp.sum(
            jnp.where(lanes == origin, jnp.broadcast_to(ids, (total, 128)), 0.0),
            axis=1,
            keepdims=True,
        )
        held = enc_ref.shape[0]
        tok = (lax.broadcasted_iota(jnp.int32, (total, held), 0) % toks).astype(jnp.float32)
        column = lax.broadcasted_iota(jnp.int32, (total, held), 1).astype(jnp.float32)
        pick = jnp.where(column == chosen * toks + tok, 1.0, 0.0).astype(jnp.bfloat16)
        for part in range(enc_width // 256):
            cols = slice(part * 256, part * 256 + 256)
            send_buf[slot, :, cols] = jnp.dot(
                pick, enc_ref[:, cols], preferred_element_type=jnp.float32
            ).astype(jnp.bfloat16)
        own = pl.ds(pl.multiple_of(me * rows, rows), rows)
        for offset in offsets:
            peer_at = flipped(me, offset)
            theirs = pl.ds(pl.multiple_of(peer_at * rows, rows), rows)
            copy = remote(
                send_buf.at[slot, theirs],
                recv_buf.at[slot, own],
                x_ssem.at[slot, offset],
                x_rsem.at[slot, offset],
                peer_at,
            )
            copy.start()
            x_copies[slot, offset] = copy
        recv_buf[slot, own, :] = send_buf[slot, own, :]

    q_copy.wait_recv()
    for part in range(width // 256):
        cols = slice(part * 256, part * 256 + 256)
        turned = pltpu.roll(q_ref[:, cols].astype(jnp.float32), 1, 0)
        first = lax.broadcasted_iota(jnp.int32, turned.shape, 0) == 0
        turned = jnp.where(first, jnp.broadcast_to(q_recv[:, cols], turned.shape), turned)
        q_shift[:, cols] = turned.astype(jnp.bfloat16)
    wk_copy.wait()
    wv_copy.wait()

    scale = 1.0 / DH**0.5
    for slot in range(2):
        for offset in offsets:
            x_copies[slot, offset].wait_recv()

        @pl.loop(0, width // 256)
        def project(tile):
            cols = pl.ds(pl.multiple_of(tile * 256, 256), 256)
            x = recv_buf[slot]
            k_buf[:, cols] = jnp.dot(
                x, wk_ref[:, cols], preferred_element_type=jnp.float32
            ).astype(jnp.bfloat16)
            v_buf[:, cols] = jnp.dot(
                x, wv_ref[:, cols], preferred_element_type=jnp.float32
            ).astype(jnp.bfloat16)

        @pl.loop(0, HEADS // 4)
        def attend(step):
            for part in range(4):
                cols = pl.ds(pl.multiple_of((step * 4 + part) * DH, DH), DH)
                query = q_shift[slot * SPAN : slot * SPAN + SPAN, cols]
                scores = (
                    lax.dot_general(
                        query,
                        k_buf[:, cols],
                        (((1,), (1,)), ((), ())),
                        preferred_element_type=jnp.float32,
                    )
                    * scale
                )
                top = jnp.max(scores, axis=1, keepdims=True)
                expo = jnp.exp(scores - top)
                weights = (expo / jnp.sum(expo, axis=1, keepdims=True)).astype(jnp.bfloat16)
                result[pl.ds(7 + slot * SPAN, SPAN), cols] = jnp.dot(
                    weights, v_buf[:, cols], preferred_element_type=jnp.float32
                )

        if slot == 0:
            row_send[...] = result[7:8, :]
            row_copy = remote(row_send, row_recv, row_ssem.at[1], row_rsem.at[1], previous)
            row_copy.start()

    row_copy.wait_recv()
    result[8 + last : 9 + last, :] = row_recv[...]
    out_ref[...] = result[8 : 9 + last, :].astype(jnp.bfloat16)
    for offset in offsets:
        id_copies[offset].wait_send()
        for slot in range(2):
            x_copies[slot, offset].wait_send()
    q_copy.wait_send()
    row_copy.wait_send()


def kernel_body(queries, encodings, neighbour_ids, lengths, w_key, w_value):
    count = lax.axis_size("seq")
    position = lax.axis_index("seq")
    tok_rows, width = queries.shape
    held, toks, enc_width = encodings.shape
    total = count * 2 * toks
    dma = pltpu.SemaphoreType.DMA
    attended = pl.pallas_call(
        functools.partial(kernel, count, toks),
        out_shape=jax.ShapeDtypeStruct((tok_rows, width), jnp.bfloat16),
        in_specs=[
            pl.BlockSpec(memory_space=pltpu.SMEM),
            pl.BlockSpec(memory_space=pltpu.VMEM),
            pl.BlockSpec(memory_space=pl.ANY),
            pl.BlockSpec(memory_space=pl.ANY),
            pl.BlockSpec(memory_space=pl.ANY),
        ],
        out_specs=pl.BlockSpec(memory_space=pltpu.VMEM),
        scratch_shapes=[
            pltpu.VMEM((held * toks, enc_width), jnp.bfloat16),
            pltpu.VMEM((enc_width, width), jnp.bfloat16),
            pltpu.VMEM((enc_width, width), jnp.bfloat16),
            pltpu.VMEM((1, 128), jnp.float32),
            pltpu.VMEM((count, 1, 128), jnp.float32),
            pltpu.VMEM((2, total, enc_width), jnp.bfloat16),
            pltpu.VMEM((2, total, enc_width), jnp.bfloat16),
            pltpu.VMEM((1, width), jnp.float32),
            pltpu.VMEM((1, width), jnp.float32),
            pltpu.VMEM((tok_rows, width), jnp.bfloat16),
            pltpu.VMEM((total, width), jnp.bfloat16),
            pltpu.VMEM((total, width), jnp.bfloat16),
            pltpu.VMEM((tok_rows + 8, width), jnp.float32),
            pltpu.VMEM((1, width), jnp.float32),
            pltpu.VMEM((1, width), jnp.float32),
            dma((3,)),
            dma((count,)),
            dma((count,)),
            dma((2, count)),
            dma((2, count)),
            dma((2,)),
            dma((2,)),
        ],
        compiler_params=pltpu.CompilerParams(
            collective_id=0, has_side_effects=True, vmem_limit_bytes=48 * 1024 * 1024
        ),
        cost_estimate=pl.CostEstimate(
            flops=8 * total * enc_width * width, bytes_accessed=10 << 20, transcendentals=0
        ),
    )(neighbour_ids, queries, encodings.reshape(held * toks, enc_width), w_key, w_value)
    slot_room = tok_rows * count // lengths.shape[0]
    global_rows = position * tok_rows + jnp.arange(tok_rows, dtype=jnp.int32)
    within = global_rows % slot_room
    prompt = global_rows // slot_room
    limit = jnp.sum(
        jnp.where(
            prompt[:, None] == jnp.arange(lengths.shape[0], dtype=jnp.int32)[None, :],
            lengths[None, :],
            0,
        ),
        axis=1,
    )
    live = (within >= 63) & (within < limit)
    return jnp.where(live[:, None], attended, 0).astype(jnp.bfloat16)


def body(queries, encodings, neighbour_ids, lengths, w_key, w_value):
    count = lax.axis_size("seq")
    held, toks, enc_width = encodings.shape
    small = count <= 32 and count & (count - 1) == 0 and held <= 256
    tiled = (2 * toks) % 16 == 0 and (held * toks) % 16 == 0
    if small and tiled and queries.shape[0] == 2 * SPAN:
        return kernel_body(queries, encodings, neighbour_ids, lengths, w_key, w_value)
    return general_body(queries, encodings, neighbour_ids, lengths, w_key, w_value)


def solution(mesh):
    in_specs = (
        P(("groups", "seq"), None),
        P("groups", "seq", None),
        P(("groups", "seq"), None),
        P("groups"),
        P(),
        P(),
    )
    out_specs = P(("groups", "seq"), None)
    return jax.shard_map(body, mesh=mesh, in_specs=in_specs, out_specs=out_specs, check_vma=False)
```

```python
import functools
import jax
import jax.numpy as jnp
from jax import lax
from jax.experimental import pallas as pl
from jax.experimental.pallas import tpu as pltpu
from jax.sharding import PartitionSpec as P

HEADS = 16
DH = 128
SPAN = 64


def general_body(queries, encodings, neighbour_ids, lengths, w_key, w_value):
    seq_count = lax.axis_size("seq")
    position = lax.axis_index("seq")
    tok_rows, width = queries.shape
    blocks = tok_rows // 64
    slots = blocks + 1
    enc_width = encodings.shape[2]
    id_all = lax.all_gather(neighbour_ids, "seq", axis=0, tiled=True)
    total_spans = id_all.shape[0]
    wanted_span = (
        jnp.arange(seq_count, dtype=jnp.int32)[:, None] * blocks
        - 1
        + jnp.arange(slots, dtype=jnp.int32)[None, :]
    )
    wanted_span = jnp.clip(wanted_span, 0, total_spans - 1)
    wanted = id_all[wanted_span].reshape(seq_count, 2 * slots)
    outgoing = encodings[wanted]
    block = lax.all_to_all(outgoing, "seq", split_axis=0, concat_axis=2, tiled=True)
    flat = block.reshape(-1, enc_width)
    shape = block.shape[:3] + (width,)
    key_rows = (
        jnp.dot(flat, w_key, preferred_element_type=jnp.float32).astype(jnp.bfloat16).reshape(shape)
    )
    value_rows = (
        jnp.dot(flat, w_value, preferred_element_type=jnp.float32)
        .astype(jnp.bfloat16)
        .reshape(shape)
    )
    ntok = key_rows.shape[2]
    key_total = key_rows.shape[1] * ntok
    key_set = key_rows.reshape(key_total, HEADS, DH)
    value_set = value_rows.reshape(key_total, HEADS, DH)
    key_slot = jnp.arange(key_total, dtype=jnp.int32) // (2 * ntok)
    local_rows = jnp.arange(tok_rows, dtype=jnp.int32)
    token_slot = (local_rows + 1) // 64
    allowed = token_slot[:, None] == key_slot[None, :]
    query_set = queries.reshape(tok_rows, HEADS, DH)
    scale = 1.0 / DH**0.5
    scores = (
        jnp.einsum("thd,khd->htk", query_set, key_set, preferred_element_type=jnp.float32) * scale
    )
    scores = jnp.where(allowed[None, :, :], scores, -1e30)
    top = jnp.max(scores, axis=2, keepdims=True)
    expo = jnp.where(allowed[None, :, :], jnp.exp(scores - top), 0.0)
    weights = (expo / jnp.sum(expo, axis=2, keepdims=True)).astype(jnp.bfloat16)
    result = jnp.einsum(
        "htk,khd->thd", weights, value_set, preferred_element_type=jnp.float32
    ).reshape(tok_rows, width)
    slot_room = tok_rows * seq_count // lengths.shape[0]
    global_rows = position * tok_rows + local_rows
    within = global_rows % slot_room
    prompt = global_rows // slot_room
    limit = jnp.sum(
        jnp.where(
            prompt[:, None] == jnp.arange(lengths.shape[0], dtype=jnp.int32)[None, :],
            lengths[None, :],
            0,
        ),
        axis=1,
    )
    live = (within >= 63) & (within < limit)
    return jnp.where(live[:, None], result, 0.0).astype(jnp.bfloat16)


def flipped(index, offset):
    bit = 1
    while bit <= offset:
        if offset & bit:
            index = index + bit - 2 * bit * ((index // bit) % 2)
        bit *= 2
    return index


def kernel(
    count,
    toks,
    ids_ref,
    lengths_ref,
    q_hbm,
    enc_hbm,
    wk_hbm,
    wv_hbm,
    out_ref,
    q_ref,
    enc_ref,
    wk_ref,
    wv_ref,
    id_send,
    id_recv,
    send_buf,
    recv_buf,
    q_send,
    q_recv,
    q_pairs,
    k_buf,
    v_buf,
    result,
    row_send,
    row_recv,
    local_sem,
    id_ssem,
    id_rsem,
    x_ssem,
    x_rsem,
    row_ssem,
    row_rsem,
):
    me = lax.axis_index("seq")
    following = lax.rem(me + 1, count)
    previous = lax.rem(me + count - 1, count)
    rows = 2 * toks
    total = count * rows
    enc_width = enc_ref.shape[1]
    tok_rows, width = q_ref.shape
    half = count // 2
    offsets = sorted(range(1, count), reverse=True)

    def local(source, target, index):
        copy = pltpu.make_async_copy(source, target, local_sem.at[index])
        copy.start()
        return copy

    def remote(source, target, send_sem, recv_sem, device):
        return pltpu.make_async_remote_copy(
            src_ref=source,
            dst_ref=target,
            send_sem=send_sem,
            recv_sem=recv_sem,
            device_id={"seq": device},
            device_id_type=pl.DeviceIdType.MESH,
        )

    barrier = pltpu.get_barrier_semaphore()
    for offset in offsets:
        pl.semaphore_signal(
            barrier,
            inc=1,
            device_id={"seq": flipped(me, offset)},
            device_id_type=pl.DeviceIdType.MESH,
        )
    q_load = local(q_hbm, q_ref, 3)
    enc_copy = local(enc_hbm, enc_ref, 0)
    wk_copy = local(wk_hbm, wk_ref, 1)
    wv_copy = local(wv_hbm, wv_ref, 2)

    lane = lax.broadcasted_iota(jnp.int32, (1, 128), 1)
    mine = jnp.zeros((1, 128), jnp.float32)
    for span in range(2):
        for which in range(2):
            value = ids_ref[span, which].astype(jnp.float32)
            mine = jnp.where(lane == me * 4 + span * 2 + which, value, mine)
    id_send[...] = mine
    id_recv[me] = mine
    last = tok_rows - 1
    q_load.wait()
    q_send[...] = q_ref[last - 15 :, :].astype(jnp.float32)[15:, :]

    pl.semaphore_wait(barrier, count - 1)

    id_copies = {}
    for offset in offsets:
        id_copies[offset] = remote(
            id_send, id_recv.at[me], id_ssem.at[offset], id_rsem.at[offset], flipped(me, offset)
        )
        id_copies[offset].start()
    q_copy = remote(q_send, q_recv, row_ssem.at[0], row_rsem.at[0], following)
    q_copy.start()
    enc_copy.wait()
    for offset in offsets:
        id_copies[offset].wait_recv()
    ids = jnp.sum(id_recv[...], axis=0)

    x_copies = {}
    own = pl.ds(pl.multiple_of(me * rows, rows), rows)
    for slot in range(2):
        for offset in offsets:
            peer_at = flipped(me, offset)
            theirs = pl.ds(pl.multiple_of(peer_at * rows, rows), rows)
            x_copies[slot, offset] = remote(
                send_buf.at[slot, theirs],
                recv_buf.at[slot, own],
                x_ssem.at[slot, offset],
                x_rsem.at[slot, offset],
                peer_at,
            )
    for slot in range(2):
        row = lax.broadcasted_iota(jnp.int32, (total, 128), 0)
        lanes = lax.broadcasted_iota(jnp.int32, (total, 128), 1)
        peer = row // rows
        which = (row % rows) // toks
        if slot == 0:
            origin = lax.rem(peer + count - 1, count) * 4 + 2 + which
        else:
            origin = peer * 4 + which
        chosen = jnp.sum(
            jnp.where(lanes == origin, jnp.broadcast_to(ids, (total, 128)), 0.0),
            axis=1,
            keepdims=True,
        )
        held = enc_ref.shape[0]
        tok = (lax.broadcasted_iota(jnp.int32, (total, held), 0) % toks).astype(jnp.float32)
        column = lax.broadcasted_iota(jnp.int32, (total, held), 1).astype(jnp.float32)
        pick = jnp.where(column == chosen * toks + tok, 1.0, 0.0).astype(jnp.bfloat16)
        for part in range(enc_width // 256):
            cols = slice(part * 256, part * 256 + 256)
            send_buf[slot, :, cols] = jnp.dot(
                pick, enc_ref[:, cols], preferred_element_type=jnp.float32
            ).astype(jnp.bfloat16)
        for offset in offsets:
            x_copies[slot, offset].start()
        recv_buf[slot, own, :] = send_buf[slot, own, :]

    q_copy.wait_recv()
    blank = jnp.zeros((SPAN, DH), jnp.bfloat16)
    for part in range(width // 256):
        cols = slice(part * 256, part * 256 + 256)
        turned = pltpu.roll(q_ref[:, cols].astype(jnp.float32), 1, 0)
        first = lax.broadcasted_iota(jnp.int32, turned.shape, 0) == 0
        turned = jnp.where(first, jnp.broadcast_to(q_recv[:, cols], turned.shape), turned)
        turned = turned.astype(jnp.bfloat16)
        for slot in range(2):
            span_rows = turned[slot * SPAN : slot * SPAN + SPAN, :]
            q_pairs[slot, part, :SPAN, :DH] = span_rows[:, :DH]
            q_pairs[slot, part, :SPAN, DH:] = blank
            q_pairs[slot, part, SPAN:, :DH] = blank
            q_pairs[slot, part, SPAN:, DH:] = span_rows[:, DH:]
    wk_copy.wait()
    wv_copy.wait()

    near = total // 2
    side = me // half
    near_rows = pl.ds(pl.multiple_of(side * near, near), near)
    far_rows = pl.ds(pl.multiple_of((1 - side) * near, near), near)

    def project(slot, source, place, cols):
        x = recv_buf[slot, source, :]
        k_buf[slot, place, cols] = jnp.dot(
            x, wk_ref[:, cols], preferred_element_type=jnp.float32
        ).astype(jnp.bfloat16)
        v_buf[slot, place, cols] = jnp.dot(
            x, wv_ref[:, cols], preferred_element_type=jnp.float32
        ).astype(jnp.bfloat16)

    factor = 1.4426950408889634 / DH**0.5

    def attend(slot, tile):
        cols = slice(tile * 256, tile * 256 + 256)
        scores = lax.dot_general(
            k_buf[slot, :, cols],
            q_pairs[slot, tile],
            (((1,), (1,)), ((), ())),
            preferred_element_type=jnp.float32,
        )
        top = jnp.max(scores, axis=0, keepdims=True)
        expo = jnp.exp2((scores - top) * factor)
        weights = (expo * (1.0 / jnp.sum(expo, axis=0, keepdims=True))).astype(jnp.bfloat16)
        both = lax.dot_general(
            weights,
            v_buf[slot, :, cols],
            (((0,), (0,)), ((), ())),
            preferred_element_type=jnp.float32,
        )
        low = 7 + slot * SPAN
        for part in range(2):
            result[low : low + SPAN, tile * 256 + part * DH : tile * 256 + part * DH + DH] = both[
                part * SPAN : part * SPAN + SPAN, part * DH : part * DH + DH
            ]

    room = tok_rows * count // lengths_ref.shape[0]
    start = me * tok_rows
    limit = lengths_ref[0]
    for index in range(1, lengths_ref.shape[0]):
        limit = jnp.where(start // room == index, lengths_ref[index], limit)

    def finish(low, high):
        within = start % room + low + lax.broadcasted_iota(jnp.int32, (high - low, 256), 0)
        live = (within >= SPAN - 1) & (within < limit)
        for part in range(width // 256):
            cols = slice(part * 256, part * 256 + 256)
            out_ref[low:high, cols] = jnp.where(
                live, result[8 + low : 8 + high, cols], 0.0
            ).astype(jnp.bfloat16)

    for slot in range(2):
        for offset in offsets:
            if offset < half:
                x_copies[slot, offset].wait_recv()

        @pl.loop(0, width // 256)
        def project_near(tile):
            project(
                slot, near_rows, slice(0, near), pl.ds(pl.multiple_of(tile * 256, 256), 256)
            )

    for slot in range(2):
        for offset in offsets:
            if offset >= half:
                x_copies[slot, offset].wait_recv()
        tiles = width // 256
        for tile in range(tiles + 1):
            if tile < tiles:
                project(
                    slot, far_rows, slice(near, total), slice(tile * 256, tile * 256 + 256)
                )
            if tile > 0:
                attend(slot, tile - 1)
        if slot == 0:
            row_send[...] = result[7:8, :]
            row_copy = remote(row_send, row_recv, row_ssem.at[1], row_rsem.at[1], previous)
            row_copy.start()
            finish(0, 48)

    row_copy.wait_recv()
    result[8 + last : 9 + last, :] = row_recv[...]
    finish(48, tok_rows)
    for offset in offsets:
        id_copies[offset].wait_send()
        x_copies[0, offset].wait_send()
        x_copies[1, offset].wait_send()
    q_copy.wait_send()
    row_copy.wait_send()


def kernel_body(queries, encodings, neighbour_ids, lengths, w_key, w_value):
    count = lax.axis_size("seq")
    tok_rows, width = queries.shape
    held, toks, enc_width = encodings.shape
    total = count * 2 * toks
    dma = pltpu.SemaphoreType.DMA
    return pl.pallas_call(
        functools.partial(kernel, count, toks),
        out_shape=jax.ShapeDtypeStruct((tok_rows, width), jnp.bfloat16),
        in_specs=[
            pl.BlockSpec(memory_space=pltpu.SMEM),
            pl.BlockSpec(memory_space=pltpu.SMEM),
            pl.BlockSpec(memory_space=pl.ANY),
            pl.BlockSpec(memory_space=pl.ANY),
            pl.BlockSpec(memory_space=pl.ANY),
            pl.BlockSpec(memory_space=pl.ANY),
        ],
        out_specs=pl.BlockSpec(memory_space=pltpu.VMEM),
        scratch_shapes=[
            pltpu.VMEM((tok_rows, width), jnp.bfloat16),
            pltpu.VMEM((held * toks, enc_width), jnp.bfloat16),
            pltpu.VMEM((enc_width, width), jnp.bfloat16),
            pltpu.VMEM((enc_width, width), jnp.bfloat16),
            pltpu.VMEM((1, 128), jnp.float32),
            pltpu.VMEM((count, 1, 128), jnp.float32),
            pltpu.VMEM((2, total, enc_width), jnp.bfloat16),
            pltpu.VMEM((2, total, enc_width), jnp.bfloat16),
            pltpu.VMEM((1, width), jnp.float32),
            pltpu.VMEM((1, width), jnp.float32),
            pltpu.VMEM((2, width // 256, 2 * SPAN, 256), jnp.bfloat16),
            pltpu.VMEM((2, total, width), jnp.bfloat16),
            pltpu.VMEM((2, total, width), jnp.bfloat16),
            pltpu.VMEM((tok_rows + 8, width), jnp.float32),
            pltpu.VMEM((1, width), jnp.float32),
            pltpu.VMEM((1, width), jnp.float32),
            dma((4,)),
            dma((count,)),
            dma((count,)),
            dma((2, count)),
            dma((2, count)),
            dma((2,)),
            dma((2,)),
        ],
        compiler_params=pltpu.CompilerParams(
            collective_id=0, has_side_effects=True, vmem_limit_bytes=62 * 1024 * 1024
        ),
        cost_estimate=pl.CostEstimate(
            flops=8 * total * enc_width * width, bytes_accessed=10 << 20, transcendentals=0
        ),
    )(neighbour_ids, lengths, queries, encodings.reshape(held * toks, enc_width), w_key, w_value)


def body(queries, encodings, neighbour_ids, lengths, w_key, w_value):
    count = lax.axis_size("seq")
    held, toks, enc_width = encodings.shape
    small = count <= 32 and count & (count - 1) == 0 and held <= 256
    tiled = (2 * toks) % 16 == 0 and (held * toks) % 16 == 0
    room = 2 * SPAN * count // lengths.shape[0]
    whole = room % (2 * SPAN) == 0
    if small and tiled and whole and queries.shape[0] == 2 * SPAN:
        return kernel_body(queries, encodings, neighbour_ids, lengths, w_key, w_value)
    return general_body(queries, encodings, neighbour_ids, lengths, w_key, w_value)


def solution(mesh):
    in_specs = (
        P(("groups", "seq"), None),
        P("groups", "seq", None),
        P(("groups", "seq"), None),
        P("groups"),
        P(),
        P(),
    )
    out_specs = P(("groups", "seq"), None)
    return jax.shard_map(body, mesh=mesh, in_specs=in_specs, out_specs=out_specs, check_vma=False)
```

```python
import functools
import jax
import jax.numpy as jnp
from jax import lax
from jax.experimental import pallas as pl
from jax.experimental.pallas import tpu as pltpu
from jax.sharding import PartitionSpec as P

HEADS = 16
DH = 128
SPAN = 64


def general_body(queries, encodings, neighbour_ids, lengths, w_key, w_value):
    seq_count = lax.axis_size("seq")
    position = lax.axis_index("seq")
    tok_rows, width = queries.shape
    blocks = tok_rows // 64
    slots = blocks + 1
    enc_width = encodings.shape[2]
    id_all = lax.all_gather(neighbour_ids, "seq", axis=0, tiled=True)
    total_spans = id_all.shape[0]
    wanted_span = (
        jnp.arange(seq_count, dtype=jnp.int32)[:, None] * blocks
        - 1
        + jnp.arange(slots, dtype=jnp.int32)[None, :]
    )
    wanted_span = jnp.clip(wanted_span, 0, total_spans - 1)
    wanted = id_all[wanted_span].reshape(seq_count, 2 * slots)
    outgoing = encodings[wanted]
    block = lax.all_to_all(outgoing, "seq", split_axis=0, concat_axis=2, tiled=True)
    flat = block.reshape(-1, enc_width)
    shape = block.shape[:3] + (width,)
    key_rows = (
        jnp.dot(flat, w_key, preferred_element_type=jnp.float32).astype(jnp.bfloat16).reshape(shape)
    )
    value_rows = (
        jnp.dot(flat, w_value, preferred_element_type=jnp.float32)
        .astype(jnp.bfloat16)
        .reshape(shape)
    )
    ntok = key_rows.shape[2]
    key_total = key_rows.shape[1] * ntok
    key_set = key_rows.reshape(key_total, HEADS, DH)
    value_set = value_rows.reshape(key_total, HEADS, DH)
    key_slot = jnp.arange(key_total, dtype=jnp.int32) // (2 * ntok)
    local_rows = jnp.arange(tok_rows, dtype=jnp.int32)
    token_slot = (local_rows + 1) // 64
    allowed = token_slot[:, None] == key_slot[None, :]
    query_set = queries.reshape(tok_rows, HEADS, DH)
    scale = 1.0 / DH**0.5
    scores = (
        jnp.einsum("thd,khd->htk", query_set, key_set, preferred_element_type=jnp.float32) * scale
    )
    scores = jnp.where(allowed[None, :, :], scores, -1e30)
    top = jnp.max(scores, axis=2, keepdims=True)
    expo = jnp.where(allowed[None, :, :], jnp.exp(scores - top), 0.0)
    weights = (expo / jnp.sum(expo, axis=2, keepdims=True)).astype(jnp.bfloat16)
    result = jnp.einsum(
        "htk,khd->thd", weights, value_set, preferred_element_type=jnp.float32
    ).reshape(tok_rows, width)
    slot_room = tok_rows * seq_count // lengths.shape[0]
    global_rows = position * tok_rows + local_rows
    within = global_rows % slot_room
    prompt = global_rows // slot_room
    limit = jnp.sum(
        jnp.where(
            prompt[:, None] == jnp.arange(lengths.shape[0], dtype=jnp.int32)[None, :],
            lengths[None, :],
            0,
        ),
        axis=1,
    )
    live = (within >= 63) & (within < limit)
    return jnp.where(live[:, None], result, 0.0).astype(jnp.bfloat16)


def flipped(index, offset):
    bit = 1
    while bit <= offset:
        if offset & bit:
            index = index + bit - 2 * bit * ((index // bit) % 2)
        bit *= 2
    return index


def kernel(
    count,
    toks,
    ids_ref,
    lengths_ref,
    q_hbm,
    enc_hbm,
    wk_hbm,
    wv_hbm,
    out_hbm,
    out_ref,
    q_ref,
    enc_ref,
    wk_ref,
    wv_ref,
    id_send,
    id_recv,
    send_buf,
    recv_buf,
    q_send,
    q_recv,
    q_pairs,
    k_buf,
    v_buf,
    result,
    row_send,
    row_recv,
    local_sem,
    id_ssem,
    id_rsem,
    x_ssem,
    x_rsem,
    row_ssem,
    row_rsem,
    out_sem,
):
    me = lax.axis_index("seq")
    following = lax.rem(me + 1, count)
    previous = lax.rem(me + count - 1, count)
    rows = 2 * toks
    total = count * rows
    enc_width = enc_ref.shape[1]
    tok_rows, width = q_ref.shape
    half = count // 2
    offsets = sorted(range(1, count), reverse=True)

    def local(source, target, index):
        copy = pltpu.make_async_copy(source, target, local_sem.at[index])
        copy.start()
        return copy

    def remote(source, target, send_sem, recv_sem, device):
        return pltpu.make_async_remote_copy(
            src_ref=source,
            dst_ref=target,
            send_sem=send_sem,
            recv_sem=recv_sem,
            device_id={"seq": device},
            device_id_type=pl.DeviceIdType.MESH,
        )

    barrier = pltpu.get_barrier_semaphore()
    for offset in offsets:
        pl.semaphore_signal(
            barrier,
            inc=1,
            device_id={"seq": flipped(me, offset)},
            device_id_type=pl.DeviceIdType.MESH,
        )
    q_load = local(q_hbm, q_ref, 3)
    enc_copy = local(enc_hbm, enc_ref, 0)
    wk_copy = local(wk_hbm, wk_ref, 1)
    wv_copy = local(wv_hbm, wv_ref, 2)

    lane = lax.broadcasted_iota(jnp.int32, (1, 128), 1)
    mine = jnp.zeros((1, 128), jnp.float32)
    for span in range(2):
        for which in range(2):
            value = ids_ref[span, which].astype(jnp.float32)
            mine = jnp.where(lane == me * 4 + span * 2 + which, value, mine)
    id_send[...] = mine
    id_recv[me] = mine
    last = tok_rows - 1
    q_load.wait()
    q_send[...] = q_ref[last - 15 :, :].astype(jnp.float32)[15:, :]

    pl.semaphore_wait(barrier, count - 1)

    id_copies = {}
    for offset in offsets:
        id_copies[offset] = remote(
            id_send, id_recv.at[me], id_ssem.at[offset], id_rsem.at[offset], flipped(me, offset)
        )
        id_copies[offset].start()
    q_copy = remote(q_send, q_recv, row_ssem.at[0], row_rsem.at[0], following)
    q_copy.start()
    enc_copy.wait()
    for offset in offsets:
        id_copies[offset].wait_recv()
    ids = jnp.sum(id_recv[...], axis=0)

    x_copies = {}
    own = pl.ds(pl.multiple_of(me * rows, rows), rows)
    for slot in range(2):
        for offset in offsets:
            peer_at = flipped(me, offset)
            theirs = pl.ds(pl.multiple_of(peer_at * rows, rows), rows)
            x_copies[slot, offset] = remote(
                send_buf.at[slot, theirs],
                recv_buf.at[slot, own],
                x_ssem.at[slot, offset],
                x_rsem.at[slot, offset],
                peer_at,
            )
    for slot in range(2):
        row = lax.broadcasted_iota(jnp.int32, (total, 128), 0)
        lanes = lax.broadcasted_iota(jnp.int32, (total, 128), 1)
        peer = row // rows
        which = (row % rows) // toks
        if slot == 0:
            origin = lax.rem(peer + count - 1, count) * 4 + 2 + which
        else:
            origin = peer * 4 + which
        chosen = jnp.sum(
            jnp.where(lanes == origin, jnp.broadcast_to(ids, (total, 128)), 0.0),
            axis=1,
            keepdims=True,
        )
        held = enc_ref.shape[0]
        tok = (lax.broadcasted_iota(jnp.int32, (total, held), 0) % toks).astype(jnp.float32)
        column = lax.broadcasted_iota(jnp.int32, (total, held), 1).astype(jnp.float32)
        pick = jnp.where(column == chosen * toks + tok, 1.0, 0.0).astype(jnp.bfloat16)
        for part in range(enc_width // 256):
            cols = slice(part * 256, part * 256 + 256)
            send_buf[slot, :, cols] = jnp.dot(
                pick, enc_ref[:, cols], preferred_element_type=jnp.float32
            ).astype(jnp.bfloat16)
        for offset in offsets:
            if offset >= half:
                x_copies[slot, offset].start()
        recv_buf[slot, own, :] = send_buf[slot, own, :]

    for slot in range(2):
        for offset in offsets:
            if offset < half:
                x_copies[slot, offset].start()

    q_copy.wait_recv()
    blank = jnp.zeros((SPAN, DH), jnp.bfloat16)
    for part in range(width // 256):
        cols = slice(part * 256, part * 256 + 256)
        turned = pltpu.roll(q_ref[:, cols].astype(jnp.float32), 1, 0)
        first = lax.broadcasted_iota(jnp.int32, turned.shape, 0) == 0
        turned = jnp.where(first, jnp.broadcast_to(q_recv[:, cols], turned.shape), turned)
        turned = turned.astype(jnp.bfloat16)
        for slot in range(2):
            span_rows = turned[slot * SPAN : slot * SPAN + SPAN, :]
            q_pairs[slot, part, :SPAN, :DH] = span_rows[:, :DH]
            q_pairs[slot, part, :SPAN, DH:] = blank
            q_pairs[slot, part, SPAN:, :DH] = blank
            q_pairs[slot, part, SPAN:, DH:] = span_rows[:, DH:]
    wk_copy.wait()
    wv_copy.wait()

    near = total // 2
    side = me // half
    near_rows = pl.ds(pl.multiple_of(side * near, near), near)
    far_rows = pl.ds(pl.multiple_of((1 - side) * near, near), near)

    def project(slot, source, place, cols):
        x = recv_buf[slot, source, :]
        k_buf[slot, place, cols] = jnp.dot(
            x, wk_ref[:, cols], preferred_element_type=jnp.float32
        ).astype(jnp.bfloat16)
        v_buf[slot, place, cols] = jnp.dot(
            x, wv_ref[:, cols], preferred_element_type=jnp.float32
        ).astype(jnp.bfloat16)

    factor = 1.4426950408889634 / DH**0.5

    def attend(slot, tile):
        cols = slice(tile * 256, tile * 256 + 256)
        scores = lax.dot_general(
            k_buf[slot, :, cols],
            q_pairs[slot, tile],
            (((1,), (1,)), ((), ())),
            preferred_element_type=jnp.float32,
        )
        top = jnp.max(scores, axis=0, keepdims=True)
        expo = jnp.exp2((scores - top) * factor)
        weights = (expo * (1.0 / jnp.sum(expo, axis=0, keepdims=True))).astype(jnp.bfloat16)
        both = lax.dot_general(
            weights,
            v_buf[slot, :, cols],
            (((0,), (0,)), ((), ())),
            preferred_element_type=jnp.float32,
        )
        low = 7 + slot * SPAN
        for part in range(2):
            result[low : low + SPAN, tile * 256 + part * DH : tile * 256 + part * DH + DH] = both[
                part * SPAN : part * SPAN + SPAN, part * DH : part * DH + DH
            ]

    room = tok_rows * count // lengths_ref.shape[0]
    start = me * tok_rows
    limit = lengths_ref[0]
    for index in range(1, lengths_ref.shape[0]):
        limit = jnp.where(start // room == index, lengths_ref[index], limit)

    tiles = width // 256
    out_copies = []

    def finish(low, high, first, stop):
        within = start % room + low + lax.broadcasted_iota(jnp.int32, (high - low, 256), 0)
        live = (within >= SPAN - 1) & (within < limit)
        for part in range(first, stop):
            cols = slice(part * 256, part * 256 + 256)
            out_ref[low:high, cols] = jnp.where(
                live, result[8 + low : 8 + high, cols], 0.0
            ).astype(jnp.bfloat16)
        block = (slice(low, high), slice(first * 256, stop * 256))
        copy = pltpu.make_async_copy(
            out_ref.at[block], out_hbm.at[block], out_sem.at[len(out_copies)]
        )
        copy.start()
        out_copies.append(copy)

    for slot in range(2):
        for offset in offsets:
            if offset < half:
                x_copies[slot, offset].wait_recv()

        @pl.loop(0, width // 256)
        def project_near(tile):
            project(
                slot, near_rows, slice(0, near), pl.ds(pl.multiple_of(tile * 256, 256), 256)
            )

    for slot in range(2):
        for offset in offsets:
            if offset >= half:
                x_copies[slot, offset].wait_recv()
        for tile in range(tiles + 2):
            if tile < tiles:
                project(
                    slot, far_rows, slice(near, total), slice(tile * 256, tile * 256 + 256)
                )
            if 0 < tile <= tiles:
                attend(slot, tile - 1)
            if slot == 1 and tile > 1:
                finish(48, tok_rows - 16, tile - 2, tile - 1)
        if slot == 0:
            row_send[...] = result[7:8, :]
            row_copy = remote(row_send, row_recv, row_ssem.at[1], row_rsem.at[1], previous)
            row_copy.start()
            finish(0, 48, 0, tiles)

    row_copy.wait_recv()
    result[8 + last : 9 + last, :] = row_recv[...]
    finish(tok_rows - 16, tok_rows, 0, tiles)
    for offset in offsets:
        id_copies[offset].wait_send()
        x_copies[0, offset].wait_send()
        x_copies[1, offset].wait_send()
    q_copy.wait_send()
    row_copy.wait_send()
    for copy in out_copies:
        copy.wait()


def kernel_body(queries, encodings, neighbour_ids, lengths, w_key, w_value):
    count = lax.axis_size("seq")
    tok_rows, width = queries.shape
    held, toks, enc_width = encodings.shape
    total = count * 2 * toks
    dma = pltpu.SemaphoreType.DMA
    return pl.pallas_call(
        functools.partial(kernel, count, toks),
        out_shape=jax.ShapeDtypeStruct((tok_rows, width), jnp.bfloat16),
        in_specs=[
            pl.BlockSpec(memory_space=pltpu.SMEM),
            pl.BlockSpec(memory_space=pltpu.SMEM),
            pl.BlockSpec(memory_space=pl.ANY),
            pl.BlockSpec(memory_space=pl.ANY),
            pl.BlockSpec(memory_space=pl.ANY),
            pl.BlockSpec(memory_space=pl.ANY),
        ],
        out_specs=pl.BlockSpec(memory_space=pl.ANY),
        scratch_shapes=[
            pltpu.VMEM((tok_rows, width), jnp.bfloat16),
            pltpu.VMEM((tok_rows, width), jnp.bfloat16),
            pltpu.VMEM((held * toks, enc_width), jnp.bfloat16),
            pltpu.VMEM((enc_width, width), jnp.bfloat16),
            pltpu.VMEM((enc_width, width), jnp.bfloat16),
            pltpu.VMEM((1, 128), jnp.float32),
            pltpu.VMEM((count, 1, 128), jnp.float32),
            pltpu.VMEM((2, total, enc_width), jnp.bfloat16),
            pltpu.VMEM((2, total, enc_width), jnp.bfloat16),
            pltpu.VMEM((1, width), jnp.float32),
            pltpu.VMEM((1, width), jnp.float32),
            pltpu.VMEM((2, width // 256, 2 * SPAN, 256), jnp.bfloat16),
            pltpu.VMEM((2, total, width), jnp.bfloat16),
            pltpu.VMEM((2, total, width), jnp.bfloat16),
            pltpu.VMEM((tok_rows + 8, width), jnp.float32),
            pltpu.VMEM((1, width), jnp.float32),
            pltpu.VMEM((1, width), jnp.float32),
            dma((4,)),
            dma((count,)),
            dma((count,)),
            dma((2, count)),
            dma((2, count)),
            dma((2,)),
            dma((2,)),
            dma((width // 256 + 2,)),
        ],
        compiler_params=pltpu.CompilerParams(
            collective_id=0, has_side_effects=True, vmem_limit_bytes=62 * 1024 * 1024
        ),
        cost_estimate=pl.CostEstimate(
            flops=8 * total * enc_width * width, bytes_accessed=10 << 20, transcendentals=0
        ),
    )(neighbour_ids, lengths, queries, encodings.reshape(held * toks, enc_width), w_key, w_value)


def body(queries, encodings, neighbour_ids, lengths, w_key, w_value):
    count = lax.axis_size("seq")
    held, toks, enc_width = encodings.shape
    small = count <= 32 and count & (count - 1) == 0 and held <= 256
    tiled = (2 * toks) % 16 == 0 and (held * toks) % 16 == 0
    room = 2 * SPAN * count // lengths.shape[0]
    whole = room % (2 * SPAN) == 0
    if small and tiled and whole and queries.shape[0] == 2 * SPAN:
        return kernel_body(queries, encodings, neighbour_ids, lengths, w_key, w_value)
    return general_body(queries, encodings, neighbour_ids, lengths, w_key, w_value)


def solution(mesh):
    in_specs = (
        P(("groups", "seq"), None),
        P("groups", "seq", None),
        P(("groups", "seq"), None),
        P("groups"),
        P(),
        P(),
    )
    out_specs = P(("groups", "seq"), None)
    return jax.shard_map(body, mesh=mesh, in_specs=in_specs, out_specs=out_specs, check_vma=False)
```
